32 devices in a mesh: dp: 4 (over y, x), ctx: 8 (over z, core).
Axes of the slice: x: 2, y: 2, z: 4, core: 2. Of those that a mesh axis runs over, the one named last changes fastest.
Arguments:
- inputs: bfloat16 [4, 8, 128, 4096], P('dp', 'ctx'), may hold values from -6 to 6
- queries: bfloat16 [4, 8, 128, 1024], P('dp', 'ctx'), may hold values from -6 to 6
- keys_values: bfloat16 [4, 8, 128, 256], P('dp', 'ctx'), may hold values from -6 to 6
- out_grad: bfloat16 [4, 8, 128, 1024], P('dp', 'ctx'), may hold values from -6 to 6
- lengths: int32 [4, 10], P('dp'), may hold values from 1 to 256, 1024 in all within a row
Outputs:
- grad_q: bfloat16 [4, 8, 128, 1024], P('dp', 'ctx')
- grad_kv: bfloat16 [4, 8, 128, 256], P('dp', 'ctx')
- grad_kv_weight: float32 [4096, 256], P('ctx')
The draws below stay inside these ranges and needn't reach their ends.
All inputs are finite; a program needn't handle non-finite values.
Results may differ from the reference program's by a relative error of at most 0.0052.
Values may be sent and summed in bfloat16 or wider, within the bound.
No kernel may reach another device: no remote copies, remote signals or barrier semaphores. Data moves between devices by JAX's collectives and lax.ppermute only.
A program may use at most 64 MiB of HBM per device.

```python
import math
import jax
import jax.numpy as jnp
import numpy as np
from jax import lax

D = 4096
HD = 128
HEADS = 8
TOK_DEV = 128
RESPONSES = 4
PIECES = 10
STRIPES = 8
LEN = 1024
ROWS = 4


def to_stripes_drawn(ordered):
    row_count = ordered.shape[0]
    feature_count = ordered.shape[2]
    return jnp.transpose(ordered.reshape(row_count, TOK_DEV, STRIPES, feature_count), (0, 2, 1, 3))


def draw_queries(key, part):
    draw_key = jax.random.fold_in(key, 11)
    entries = jnp.clip(jax.random.normal(draw_key, (ROWS, LEN, HEADS, HD), jnp.float32), -5.0, 5.0)
    return to_stripes_drawn(entries.reshape(ROWS, LEN, HEADS * HD)).astype(jnp.bfloat16)


def draw_keys_values(key, part):
    draw_key = jax.random.fold_in(key, 12)
    key_draw, value_draw = jax.random.split(draw_key, 2)
    key_part = jnp.clip(jax.random.normal(key_draw, (ROWS, LEN, HD), jnp.float32), -5.0, 5.0)
    value_part = jnp.clip(jax.random.normal(value_draw, (ROWS, LEN, HD), jnp.float32), -5.0, 5.0)
    return to_stripes_drawn(jnp.concatenate([key_part, value_part], axis=2)).astype(jnp.bfloat16)


def spiked(values, stream_key, source, target, shards_of, factor):
    def block_of(position):
        return (jnp.arange(values.shape[position]) // (values.shape[position] // shards_of)).reshape((-1,) + (1,) * (values.ndim - 1 - position))

    first = jax.random.permutation(stream_key, shards_of)[block_of(target)]
    second = (block_of(target) + shards_of // 2) % shards_of
    return jnp.where((block_of(source) == first) | (block_of(source) == second), factor * values, values)


def levels(stream_key, extent, shards, low, high):
    loudness, own = 1.0, jax.random.fold_in(stream_key, 6)
    for axis_at, parts in shards:
        heights = jnp.exp(jax.random.uniform(jax.random.fold_in(own, axis_at), (parts,), jnp.float32, low / len(shards), high / len(shards)))
        loudness = loudness * jnp.repeat(heights, extent[axis_at] // parts).reshape([-1 if axis == axis_at else 1 for axis in range(len(extent))])
    return loudness


def length_profile(amount, total, reach, slope):
    portions = [(1 << 20) // math.isqrt(standing ** slope) + 1 for standing in range(2, amount + 1)]
    rest, counts = total - reach - (amount - 1), [1] * (amount - 1)
    while rest > 0:
        candidates = [i for i in range(amount - 1) if counts[i] < reach]
        whole, budget = sum([portions[i] for i in candidates]), rest
        for i in candidates:
            extra = min(reach - counts[i], max(1, budget * portions[i] // whole), rest)
            counts[i] = counts[i] + extra
            rest = rest - extra
    return np.array([reach] + counts)


def uneven_parts(rng, count, total, limit, lean):
    if count == 2:
        one = jax.random.randint(rng, (), max(1, total - limit), min(limit, total - 1) + 1)
        return jnp.stack([one, total - one])
    tallies = jnp.asarray(length_profile(count, total, limit, lean), jnp.int32)
    pairs = (count - 1) // 2
    source_of, receiver = tallies[1:1 + 2 * pairs:2], tallies[2:2 + 2 * pairs:2]
    slack = jnp.minimum(source_of - 1, limit - receiver)
    passed = jax.random.randint(jax.random.fold_in(rng, 1), (pairs,), 0, 1 << 20) % (slack + 1)
    tallies = tallies.at[1:1 + 2 * pairs:2].set(source_of - passed).at[2:2 + 2 * pairs:2].set(receiver + passed)
    return tallies[jax.random.permutation(jax.random.fold_in(rng, 2), count)]


def gaussian(key, dims, width, limit, cuts=(), kind=jnp.bfloat16):
    values = width * jax.random.normal(key, dims, jnp.float32)
    if cuts:
        values = values * levels(key, dims, cuts, -0.22, 0.18)
    return jnp.clip(values, -limit, limit).astype(kind)


def noise_with(rng, shape, width, reach, shards, heavy, held_as=jnp.bfloat16):
    values = width * jax.random.normal(rng, shape, jnp.float32)
    if shards:
        values = values * levels(rng, shape, shards, -0.22, 0.18)
    return jnp.clip(spiked(values, jax.random.fold_in(rng, 3), *heavy), -reach, reach).astype(held_as)


def setup_inputs(seed: int = 0) -> dict:
    splits = jax.random.split(jax.random.key(seed), 6)
    return {
        "inputs": noise_with(splits[0], (ROWS, STRIPES, TOK_DEV, D), 1.0, 6.0, ((0, 4), (1, 8)), (1, 3, 8, 2.0)),
        "queries": draw_queries(jax.random.fold_in(splits[5], 71), 0),
        "keys_values": draw_keys_values(jax.random.fold_in(splits[5], 71), 0),
        "out_grad": gaussian(splits[3], (ROWS, STRIPES, TOK_DEV, HEADS * HD), 1.0, 6.0, ((0, 4), (1, 8))),
        "lengths": jax.vmap(lambda own: uneven_parts(own, PIECES, LEN, LEN // 4, 1))(jax.random.split(splits[4], ROWS)).reshape((ROWS, PIECES)).astype(jnp.int32),
    }


neg_fill = -1e30


def to_positions(banded):
    row_count, stripe_count, local_count, feature_count = banded.shape
    return jnp.transpose(banded, (0, 2, 1, 3)).reshape(row_count, stripe_count * local_count, feature_count)


def to_stripes(ordered, stripe_count):
    row_count, length_all, feature_count = ordered.shape
    return jnp.transpose(ordered.reshape(row_count, length_all // stripe_count, stripe_count, feature_count), (0, 2, 1, 3))


def piece_of(positions, piece_ends):
    return jnp.sum((positions[:, None] >= piece_ends[None, :]).astype(jnp.int32), axis=1)


def allowed_pairs(query_pos, key_pos, piece_ends):
    per_group = RESPONSES + 1
    query_piece = piece_of(query_pos, piece_ends)
    key_piece = piece_of(key_pos, piece_ends)
    same_group = (query_piece // per_group)[:, None] == (key_piece // per_group)[None, :]
    visible = ((key_piece % per_group) == 0)[None, :] | (query_piece[:, None] == key_piece[None, :])
    return (key_pos[None, :] <= query_pos[:, None]) & same_group & visible


def row_backward(q_row, kv_row, grad_row, length_row):
    positions = jnp.arange(LEN, dtype=jnp.int32)
    piece_ends = jnp.cumsum(length_row, dtype=jnp.int32)
    key_part = kv_row[:, :HD]
    value_part = kv_row[:, HD:]
    score_scale = HD ** -0.5
    block_len = min(LEN, 512)
    block_count = LEN // block_len

    def one_block(key_grads, block_index):
        first_pos = block_index * block_len
        q_block = lax.dynamic_slice_in_dim(q_row, first_pos, block_len, 0).reshape(block_len * HEADS, HD)
        grad_block = lax.dynamic_slice_in_dim(grad_row, first_pos, block_len, 0).reshape(block_len * HEADS, HD)
        query_pos = first_pos + jnp.arange(block_len, dtype=jnp.int32)
        allowed = allowed_pairs(query_pos, positions, piece_ends)
        allowed = jnp.broadcast_to(allowed[:, None, :], (block_len, HEADS, LEN)).reshape(block_len * HEADS, LEN)
        scores = jnp.dot(q_block, key_part.T, preferred_element_type=jnp.float32) * score_scale
        row_max = jnp.max(jnp.where(allowed, scores, neg_fill), axis=1, keepdims=True)
        row_sum = jnp.sum(jnp.where(allowed, jnp.exp(scores - row_max), 0.0), axis=1, keepdims=True)
        log_total = row_max + jnp.log(row_sum)
        soft_probs = jnp.where(allowed, jnp.exp(scores - log_total), 0.0)
        prob_grad = jnp.dot(grad_block, value_part.T, preferred_element_type=jnp.float32)
        row_delta = jnp.sum(soft_probs * prob_grad, axis=1, keepdims=True)
        score_grad = soft_probs * (prob_grad - row_delta)
        low_probs = soft_probs.astype(jnp.bfloat16)
        low_score = score_grad.astype(jnp.bfloat16)
        grad_q = jnp.dot(low_score, key_part, preferred_element_type=jnp.float32) * score_scale
        grad_q = grad_q.astype(jnp.bfloat16).reshape(block_len, HEADS * HD)
        key_term = jnp.dot(low_score.T, q_block, preferred_element_type=jnp.float32) * score_scale
        value_term = jnp.dot(low_probs.T, grad_block, preferred_element_type=jnp.float32)
        return key_grads + jnp.concatenate([key_term, value_term], axis=1), grad_q

    key_grads, grad_blocks = lax.scan(one_block, jnp.zeros((LEN, 2 * HD), jnp.float32), jnp.arange(block_count, dtype=jnp.int32))
    return grad_blocks.reshape(LEN, HEADS * HD), key_grads.astype(jnp.bfloat16)


def reference(inputs, queries, keys_values, out_grad, lengths):
    stripe_count = queries.shape[1]
    input_pos = to_positions(inputs)
    query_rows = to_positions(queries)
    kv_rows = to_positions(keys_values)
    grad_rows = to_positions(out_grad)
    grad_q_list = []
    grad_kv_list = []
    weight_total = jnp.zeros((D, 2 * HD), jnp.float32)
    for row_index in range(ROWS):
        grad_q_row, grad_kv_row = row_backward(query_rows[row_index], kv_rows[row_index], grad_rows[row_index], lengths[row_index])
        grad_q_list.append(grad_q_row)
        grad_kv_list.append(grad_kv_row)
        weight_total = weight_total + jnp.dot(input_pos[row_index].T, grad_kv_row, preferred_element_type=jnp.float32)
    grad_q = to_stripes(jnp.stack(grad_q_list), stripe_count)
    grad_kv = to_stripes(jnp.stack(grad_kv_list), stripe_count)
    return grad_q, grad_kv, weight_total / ROWS
```

```python
import functools

import jax
import jax.numpy as jnp
from jax import lax
from jax.experimental import pallas as pl
from jax.experimental.pallas import tpu as pltpu
from jax.sharding import PartitionSpec as P

HD = 128
RESPONSES = 4
LOG2E = 1.4426950408889634
NEG = -1e30

NT = (((1,), (1,)), ((), ()))
TN = (((0,), (0,)), ((), ()))


def dot(a, b, dims=(((1,), (0,)), ((), ()))):
    return lax.dot_general(a, b, dims, preferred_element_type=jnp.float32)


def swap(x, axis, mask):
    size = lax.axis_size(axis)
    return lax.ppermute(x, axis, [(i, i ^ mask) for i in range(size)])


def attention_kernel(half, local, pieces, *refs):
    (len_ref, me_ref), kv_refs = refs[:2], refs[2 : 2 + half + 1]
    q_ref, do_ref = refs[3 + half : 5 + half]
    gq_ref, own_ref, sib_ref = refs[5 + half : 8 + half]
    k_all, v_all, bias, x_buf, dp_buf, p_buf, ds_buf = refs[8 + half :]
    stripes = 2 * half
    me = me_ref[0]
    heads = q_ref.shape[1] // HD
    per_group = RESPONSES + 1
    coef = HD**-0.5 * LOG2E

    for k in range(half):
        rows = slice(k * local, (k + 1) * local)
        k_all[rows, :] = kv_refs[k][:, :HD]
        v_all[rows, :] = kv_refs[k][:, HD:]
    k_all[half * local :, :] = kv_refs[half][:, :HD]
    v_all[half * local :, :] = kv_refs[half][:, HD:]

    q_pos = lax.broadcasted_iota(jnp.int32, (1, local), 1) * stripes + me
    own_start = jnp.zeros((1, local), jnp.int32)
    prompt_start = jnp.zeros((1, local), jnp.int32)
    prompt_end = jnp.zeros((1, local), jnp.int32)
    start = jnp.int32(0)
    for k in range(pieces):
        length = len_ref[0, k]
        inside = q_pos >= start
        own_start = jnp.where(inside, start, own_start)
        if k % per_group == 0:
            prompt_start = jnp.where(inside, start, prompt_start)
            prompt_end = jnp.where(inside, start + length, prompt_end)
        start = start + length
    prompt_end = jnp.minimum(prompt_end, q_pos + 1)
    row_pos = lax.broadcasted_iota(jnp.int32, (local, local), 0) * stripes
    for m in range(stripes):
        b, k = m // half, m % half
        k_pos = row_pos + (me ^ (2 * k + b))
        ok = ((k_pos >= own_start) & (k_pos <= q_pos)) | (
            (k_pos >= prompt_start) & (k_pos < prompt_end)
        )
        bias[m * local : (m + 1) * local, :] = jnp.where(ok, 0.0, NEG)

    def head_pair(hp, _):
        c0 = pl.multiple_of(hp * 2 * HD, 2 * HD)
        q2 = jnp.concatenate(
            [q_ref[:, pl.ds(c0, HD)], q_ref[:, pl.ds(c0 + HD, HD)]], axis=0
        )
        do2 = jnp.concatenate(
            [do_ref[:, pl.ds(c0, HD)], do_ref[:, pl.ds(c0 + HD, HD)]], axis=0
        )
        width = 2 * local
        top = jnp.full((8, width), NEG, jnp.float32)
        for m in range(stripes):
            rows = slice(m * local, (m + 1) * local)
            b = bias[rows, :]
            x = dot(k_all[rows, :], q2, NT) + jnp.concatenate([b, b], axis=1)
            x_buf[rows, :] = x
            top = jnp.maximum(top, jnp.max(x.reshape(local // 8, 8, width), axis=0))
        top = jnp.max(top, axis=0, keepdims=True) * coef
        total = jnp.zeros((8, width), jnp.float32)
        weighted = jnp.zeros((8, width), jnp.float32)
        for m in range(stripes):
            rows = slice(m * local, (m + 1) * local)
            e = jnp.exp2(x_buf[rows, :] * coef - top)
            d = dot(v_all[rows, :], do2, NT)
            total = total + jnp.sum(e.reshape(local // 8, 8, width), axis=0)
            weighted = weighted + jnp.sum((e * d).reshape(local // 8, 8, width), axis=0)
            x_buf[rows, :] = e
            dp_buf[rows, :] = d
        total = jnp.sum(total, axis=0, keepdims=True)
        weighted = jnp.sum(weighted, axis=0, keepdims=True)
        inv = 1.0 / total
        delta = weighted * inv
        for m in range(stripes):
            rows = slice(m * local, (m + 1) * local)
            p = x_buf[rows, :] * inv
            ds = p * (dp_buf[rows, :] - delta)
            p_buf[rows, pl.ds(c0, 2 * HD)] = p.astype(jnp.bfloat16)
            ds_buf[rows, pl.ds(c0, 2 * HD)] = ds.astype(jnp.bfloat16)
        gq = dot(ds_buf[:, pl.ds(c0, 2 * HD)], k_all[...], TN) * HD**-0.5
        gq = gq.astype(jnp.bfloat16)
        gq_ref[:, pl.ds(c0, HD)] = gq[:local]
        gq_ref[:, pl.ds(c0 + HD, HD)] = gq[local:]
        return 0

    lax.fori_loop(0, heads // 2, head_pair, 0)

    q_rows = jnp.concatenate([q_ref[:, h * HD : (h + 1) * HD] for h in range(heads)], axis=0)
    do_rows = jnp.concatenate([do_ref[:, h * HD : (h + 1) * HD] for h in range(heads)], axis=0)
    half_rows = half * local
    sib_ref[:, :HD] = (dot(ds_buf[half_rows:, :], q_rows) * HD**-0.5).astype(sib_ref.dtype)
    sib_ref[:, HD:] = dot(p_buf[half_rows:, :], do_rows).astype(sib_ref.dtype)
    own_ref[:, :HD] = dot(ds_buf[:half_rows, :], q_rows) * HD**-0.5
    own_ref[:, HD:] = dot(p_buf[:half_rows, :], do_rows)


def attention(lengths, me, kv_blocks, q, do):
    half = len(kv_blocks) - 1
    local, width = q.shape
    keys = 2 * half * local
    heads = width // HD
    vm = pl.BlockSpec(memory_space=pltpu.VMEM)
    sm = pl.BlockSpec(memory_space=pltpu.SMEM)
    return pl.pallas_call(
        functools.partial(attention_kernel, half, local, lengths.shape[1]),
        out_shape=(
            jax.ShapeDtypeStruct((local, width), jnp.bfloat16),
            jax.ShapeDtypeStruct((half * local, 2 * HD), jnp.float32),
            jax.ShapeDtypeStruct((half * local, 2 * HD), jnp.bfloat16),
        ),
        in_specs=[sm, sm] + [vm] * (half + 3),
        out_specs=(vm, vm, vm),
        scratch_shapes=[
            pltpu.VMEM((keys, HD), jnp.bfloat16),
            pltpu.VMEM((keys, HD), jnp.bfloat16),
            pltpu.VMEM((keys, local), jnp.float32),
            pltpu.VMEM((keys, 2 * local), jnp.float32),
            pltpu.VMEM((keys, 2 * local), jnp.float32),
            pltpu.VMEM((keys, heads * local), jnp.bfloat16),
            pltpu.VMEM((keys, heads * local), jnp.bfloat16),
        ],
        compiler_params=pltpu.CompilerParams(vmem_limit_bytes=56 * 1024 * 1024),
    )(lengths, me, *kv_blocks, q, do)


def on_device(inputs, queries, keys_values, out_grad, lengths):
    stripes = lax.axis_size("ctx")
    rows = lax.axis_size("dp")
    half = stripes // 2
    me = lax.axis_index("ctx")
    row = lax.axis_index("dp")
    x = inputs[0, 0]
    q = queries[0, 0]
    do = out_grad[0, 0]
    kv = keys_values[0, 0]
    local, features = x.shape
    part = features // (stripes * rows)

    kv_own = [kv] + [swap(kv, "ctx", 2 * k) for k in range(1, half)]
    kv_sib = swap(jnp.concatenate(kv_own, axis=0), "ctx", 1)

    xb = x.reshape(local, stripes, rows, part)
    x_slabs = []
    for k in range(rows):
        slab = lax.dynamic_index_in_dim(xb, row ^ k, 2, keepdims=False)
        slab = slab.reshape(local, stripes * part)
        x_slabs.append(slab if k == 0 else swap(slab, "dp", k))

    gq, part_own, part_sib = attention(
        lengths, me.reshape(1).astype(jnp.int32), kv_own + [kv_sib], q, do
    )

    chip = part_own + swap(part_sib, "ctx", 1).astype(jnp.float32)
    chip = chip.reshape(half, local, 2 * HD)
    terms = [swap(chip[k].astype(jnp.bfloat16), "ctx", 2 * k) for k in range(1, half)]
    gkv = chip[0] + sum(t.astype(jnp.float32) for t in terms)
    gkv = gkv.astype(jnp.bfloat16)

    g_rows = [gkv] + [swap(gkv, "dp", k) for k in range(1, rows)]
    x_all = jnp.concatenate(x_slabs, axis=0)
    g_all = jnp.concatenate(g_rows, axis=0)
    w = dot(x_all, g_all, TN) * (1.0 / rows)
    w = w.reshape(half, 2, part, 2 * HD)
    core = me % 2
    w_own = lax.dynamic_index_in_dim(w, core, 1, keepdims=False)
    w_sib = lax.dynamic_index_in_dim(w, 1 - core, 1, keepdims=False)
    w_chip = w_own + swap(w_sib.astype(jnp.bfloat16), "ctx", 1).astype(jnp.float32)
    z = me // 2
    w_mine = lax.dynamic_index_in_dim(w_chip, z, 0, keepdims=False)
    for k in range(1, half):
        block = lax.dynamic_index_in_dim(w_chip, z ^ k, 0, keepdims=False)
        w_mine = w_mine + swap(block.astype(jnp.bfloat16), "ctx", 2 * k).astype(jnp.float32)

    low = w_mine.astype(jnp.bfloat16)
    stacked = jnp.stack([low] + [swap(low, "dp", k) for k in range(1, rows)])
    order = jnp.arange(rows) ^ row
    w_out = stacked[order].reshape(rows * part, 2 * HD).astype(jnp.float32)
    return (
        gq.reshape(1, 1, local, -1),
        gkv.reshape(1, 1, local, 2 * HD),
        w_out,
    )


def solution(mesh):
    spec = P("dp", "ctx", None, None)
    return jax.shard_map(
        on_device,
        mesh=mesh,
        in_specs=(spec, spec, spec, spec, P("dp", None)),
        out_specs=(spec, spec, P("ctx", None)),
        check_vma=False,
    )
```

```python
import functools

import jax
import jax.numpy as jnp
from jax import lax
from jax.experimental import pallas as pl
from jax.experimental.pallas import tpu as pltpu
from jax.sharding import PartitionSpec as P

HD = 128
RESPONSES = 4
LOG2E = 1.4426950408889634
NEG = -1e30

NT = (((1,), (1,)), ((), ()))
TN = (((0,), (0,)), ((), ()))


def dot(a, b, dims=(((1,), (0,)), ((), ()))):
    return lax.dot_general(a, b, dims, preferred_element_type=jnp.float32)


def swap(x, axis, mask):
    size = lax.axis_size(axis)
    return lax.ppermute(x, axis, [(i, i ^ mask) for i in range(size)])


def attention_kernel(half, local, pieces, *refs):
    stripes = 2 * half
    (len_ref, me_ref), kv_refs = refs[:2], refs[2 : 2 + stripes]
    q_ref, do_ref, gq_ref, own_ref, sib_ref = refs[2 + stripes : 7 + stripes]
    k_all, v_all, bias, x_bufs, dp_bufs, p_buf, ds_buf = refs[7 + stripes :]
    me = me_ref[0]
    heads = q_ref.shape[1] // HD
    per_group = RESPONSES + 1
    coef = HD**-0.5 * LOG2E

    for k in range(stripes):
        rows = slice(k * local, (k + 1) * local)
        k_all[rows, :] = kv_refs[k][:, :HD]
        v_all[rows, :] = kv_refs[k][:, HD:]

    q_pos = lax.broadcasted_iota(jnp.int32, (1, local), 1) * stripes + me
    own_start = jnp.zeros((1, local), jnp.int32)
    prompt_start = jnp.zeros((1, local), jnp.int32)
    prompt_end = jnp.zeros((1, local), jnp.int32)
    start = jnp.int32(0)
    for k in range(pieces):
        length = len_ref[0, k]
        inside = q_pos >= start
        own_start = jnp.where(inside, start, own_start)
        if k % per_group == 0:
            prompt_start = jnp.where(inside, start, prompt_start)
            prompt_end = jnp.where(inside, start + length, prompt_end)
        start = start + length
    prompt_end = jnp.minimum(prompt_end, q_pos + 1)
    row_pos = lax.broadcasted_iota(jnp.int32, (local, local), 0) * stripes
    for m in range(stripes):
        b, k = m // half, m % half
        k_pos = row_pos + (me ^ (2 * k + b))
        ok = ((k_pos >= own_start) & (k_pos <= q_pos)) | (
            (k_pos >= prompt_start) & (k_pos < prompt_end)
        )
        bias[m * local : (m + 1) * local, :] = jnp.where(ok, 0.0, NEG)

    def head_pair(hp, _):
        c0 = hp * 2 * HD
        x_buf = x_bufs.at[hp]
        dp_buf = dp_bufs.at[hp]
        q2 = jnp.concatenate(
            [q_ref[:, pl.ds(c0, HD)], q_ref[:, pl.ds(c0 + HD, HD)]], axis=0
        )
        do2 = jnp.concatenate(
            [do_ref[:, pl.ds(c0, HD)], do_ref[:, pl.ds(c0 + HD, HD)]], axis=0
        )
        width = 2 * local
        top = jnp.full((8, width), NEG, jnp.float32)
        for m in range(stripes):
            rows = slice(m * local, (m + 1) * local)
            b = bias[rows, :]
            x = dot(k_all[rows, :], q2, NT) + jnp.concatenate([b, b], axis=1)
            x_buf[rows, :] = x
            top = jnp.maximum(top, jnp.max(x.reshape(local // 8, 8, width), axis=0))
        top = jnp.max(top, axis=0, keepdims=True) * coef
        total = jnp.zeros((8, width), jnp.float32)
        weighted = jnp.zeros((8, width), jnp.float32)
        for m in range(stripes):
            rows = slice(m * local, (m + 1) * local)
            e = jnp.exp2(x_buf[rows, :] * coef - top)
            d = dot(v_all[rows, :], do2, NT)
            total = total + jnp.sum(e.reshape(local // 8, 8, width), axis=0)
            weighted = weighted + jnp.sum((e * d).reshape(local // 8, 8, width), axis=0)
            x_buf[rows, :] = e
            dp_buf[rows, :] = d
        total = jnp.sum(total, axis=0, keepdims=True)
        weighted = jnp.sum(weighted, axis=0, keepdims=True)
        inv = 1.0 / total
        delta = weighted * inv
        for m in range(stripes):
            rows = slice(m * local, (m + 1) * local)
            p = x_buf[rows, :] * inv
            ds = p * (dp_buf[rows, :] - delta)
            p_buf[rows, pl.ds(c0, 2 * HD)] = p.astype(jnp.bfloat16)
            ds_buf[rows, pl.ds(c0, 2 * HD)] = ds.astype(jnp.bfloat16)
        return 0

    for hp in range(heads // 2):
        head_pair(hp, 0)

    gq = (dot(k_all[...].T, ds_buf[...]).T * HD**-0.5).astype(jnp.bfloat16)
    for h in range(heads):
        gq_ref[:, h * HD : (h + 1) * HD] = gq[h * local : (h + 1) * local]
    q_rows = jnp.concatenate([q_ref[:, h * HD : (h + 1) * HD] for h in range(heads)], axis=0)
    do_rows = jnp.concatenate([do_ref[:, h * HD : (h + 1) * HD] for h in range(heads)], axis=0)
    half_rows = half * local
    sib_ref[:, :HD] = (dot(ds_buf[half_rows:, :], q_rows) * HD**-0.5).astype(sib_ref.dtype)
    sib_ref[:, HD:] = dot(p_buf[half_rows:, :], do_rows).astype(sib_ref.dtype)
    own_ref[:, :HD] = dot(ds_buf[:half_rows, :], q_rows) * HD**-0.5
    own_ref[:, HD:] = dot(p_buf[:half_rows, :], do_rows)


def attention(lengths, me, kv_blocks, q, do):
    half = len(kv_blocks) // 2
    local, width = q.shape
    keys = 2 * half * local
    heads = width // HD
    vm = pl.BlockSpec(memory_space=pltpu.VMEM)
    sm = pl.BlockSpec(memory_space=pltpu.SMEM)
    return pl.pallas_call(
        functools.partial(attention_kernel, half, local, lengths.shape[1]),
        out_shape=(
            jax.ShapeDtypeStruct((local, width), jnp.bfloat16),
            jax.ShapeDtypeStruct((half * local, 2 * HD), jnp.float32),
            jax.ShapeDtypeStruct((half * local, 2 * HD), jnp.bfloat16),
        ),
        in_specs=[sm, sm] + [vm] * (2 * half + 2),
        out_specs=(vm, vm, vm),
        scratch_shapes=[
            pltpu.VMEM((keys, HD), jnp.bfloat16),
            pltpu.VMEM((keys, HD), jnp.bfloat16),
            pltpu.VMEM((keys, local), jnp.float32),
            pltpu.VMEM((heads // 2, keys, 2 * local), jnp.float32),
            pltpu.VMEM((heads // 2, keys, 2 * local), jnp.float32),
            pltpu.VMEM((keys, heads * local), jnp.bfloat16),
            pltpu.VMEM((keys, heads * local), jnp.bfloat16),
        ],
        cost_estimate=pl.CostEstimate(flops=1000000000, bytes_accessed=0, transcendentals=0),
        compiler_params=pltpu.CompilerParams(vmem_limit_bytes=keys * 24 * 1024),
    )(lengths, me, *kv_blocks, q, do)


def on_device(inputs, queries, keys_values, out_grad, lengths):
    stripes = lax.axis_size("ctx")
    rows = lax.axis_size("dp")
    half = stripes // 2
    me = lax.axis_index("ctx")
    row = lax.axis_index("dp")
    x = inputs[0, 0]
    q = queries[0, 0]
    do = out_grad[0, 0]
    kv = keys_values[0, 0]
    local, features = x.shape
    part = features // (stripes * rows)

    kv_own = [kv] + [swap(kv, "ctx", 2 * k) for k in range(1, half)]
    kv_sib = [swap(block, "ctx", 1) for block in kv_own]

    xb = x.reshape(local, stripes, rows, part)
    x_slabs = []
    for k in range(rows):
        slab = lax.dynamic_index_in_dim(xb, row ^ k, 2, keepdims=False)
        slab = slab.reshape(local, stripes * part)
        x_slabs.append(slab if k == 0 else swap(slab, "dp", k))

    gq, part_own, part_sib = attention(
        lengths, me.reshape(1).astype(jnp.int32), kv_own + kv_sib, q, do
    )

    part_sib, x_slabs = lax.optimization_barrier((part_sib, x_slabs))

    chip = part_own + swap(part_sib, "ctx", 1).astype(jnp.float32)
    chip = chip.reshape(half, local, 2 * HD)
    terms = [swap(chip[k].astype(jnp.bfloat16), "ctx", 2 * k) for k in range(1, half)]
    gkv = chip[0] + sum(t.astype(jnp.float32) for t in terms)
    gkv = gkv.astype(jnp.bfloat16)

    g_rows = [gkv] + [swap(gkv, "dp", k) for k in range(1, rows)]
    x_all = jnp.concatenate(x_slabs, axis=0)
    g_all = jnp.concatenate(g_rows, axis=0)
    w = dot(x_all, g_all, TN) * (1.0 / rows)
    w = w.reshape(half, 2, part, 2 * HD)
    core = me % 2
    w_own = lax.dynamic_index_in_dim(w, core, 1, keepdims=False)
    w_sib = lax.dynamic_index_in_dim(w, 1 - core, 1, keepdims=False)
    w_chip = w_own + swap(w_sib.astype(jnp.bfloat16), "ctx", 1).astype(jnp.float32)
    z = me // 2
    w_mine = lax.dynamic_index_in_dim(w_chip, z, 0, keepdims=False)
    for k in range(1, half):
        block = lax.dynamic_index_in_dim(w_chip, z ^ k, 0, keepdims=False)
        w_mine = w_mine + swap(block.astype(jnp.bfloat16), "ctx", 2 * k).astype(jnp.float32)

    low = w_mine.astype(jnp.bfloat16)
    blocks = [low] + [swap(low, "dp", k) for k in range(1, rows)]
    bit = 1
    while bit < rows:
        flip = (row & bit) != 0
        blocks = [jnp.where(flip, blocks[j ^ bit], blocks[j]) for j in range(rows)]
        bit *= 2
    w_out = jnp.concatenate([b.astype(jnp.float32) for b in blocks], axis=0)
    return (
        gq.reshape(1, 1, local, -1),
        gkv.reshape(1, 1, local, 2 * HD),
        w_out,
    )


def solution(mesh):
    spec = P("dp", "ctx", None, None)
    return jax.shard_map(
        on_device,
        mesh=mesh,
        in_specs=(spec, spec, spec, spec, P("dp", None)),
        out_specs=(spec, spec, P("ctx", None)),
        check_vma=False,
    )
```

```python
import functools

import jax
import jax.numpy as jnp
from jax import lax
from jax.experimental import pallas as pl
from jax.experimental.pallas import tpu as pltpu
from jax.sharding import PartitionSpec as P

HD = 128
RESPONSES = 4
LOG2E = 1.4426950408889634
NEG = -1e30
SCALE = HD**-0.5

NT = (((1,), (1,)), ((), ()))
TN = (((0,), (0,)), ((), ()))


def dot(a, b, dims=(((1,), (0,)), ((), ()))):
    return lax.dot_general(a, b, dims, preferred_element_type=jnp.float32)


def swap(x, axis, mask):
    size = lax.axis_size(axis)
    return lax.ppermute(x, axis, [(i, i ^ mask) for i in range(size)])


def fold(x):
    return x.reshape(x.shape[0] // 8, 8, x.shape[1])


def scores_kernel(half, local, pieces, *refs):
    (len_ref, me_ref), kv_refs = refs[:2], refs[2 : 2 + half]
    q_refs, do_refs = refs[2 + half : 4 + half], refs[4 + half : 6 + half]
    e_ref, d_ref, stat_ref, q_rows, do_rows, bias = refs[6 + half :]
    stripes = 2 * half
    me = me_ref[0]
    heads = q_refs[0].shape[1] // HD
    per_group = RESPONSES + 1
    coef = SCALE * LOG2E
    width = 2 * local

    row_pos = lax.broadcasted_iota(jnp.int32, (local, local), 0) * stripes
    for b in range(2):
        q_pos = lax.broadcasted_iota(jnp.int32, (1, local), 1) * stripes + (me ^ b)
        own_start = jnp.zeros((1, local), jnp.int32)
        prompt_start = jnp.zeros((1, local), jnp.int32)
        prompt_end = jnp.zeros((1, local), jnp.int32)
        start = jnp.int32(0)
        for k in range(pieces):
            length = len_ref[0, k]
            inside = q_pos >= start
            own_start = jnp.where(inside, start, own_start)
            if k % per_group == 0:
                prompt_start = jnp.where(inside, start, prompt_start)
                prompt_end = jnp.where(inside, start + length, prompt_end)
            start = start + length
        prompt_end = jnp.minimum(prompt_end, q_pos + 1)
        for k in range(half):
            k_pos = row_pos + (me ^ (2 * k))
            ok = ((k_pos >= own_start) & (k_pos <= q_pos)) | (
                (k_pos >= prompt_start) & (k_pos < prompt_end)
            )
            bias[b, k * local : (k + 1) * local, :] = jnp.where(ok, 0.0, NEG)

    for b in range(2):
        for pair in range(heads // 2):
            c = pair * 2 * HD
            cols = slice((b * heads + 2 * pair) * local, (b * heads + 2 * pair + 2) * local)
            q2 = jnp.concatenate(
                [q_refs[b][:, c : c + HD], q_refs[b][:, c + HD : c + 2 * HD]], axis=0
            )
            do2 = jnp.concatenate(
                [do_refs[b][:, c : c + HD], do_refs[b][:, c + HD : c + 2 * HD]], axis=0
            )
            q_rows[cols, :] = q2
            do_rows[cols, :] = do2
            top = jnp.full((8, width), NEG, jnp.float32)
            for k in range(half):
                rows = slice(k * local, (k + 1) * local)
                add = bias[b, rows, :]
                x = dot(kv_refs[k][:, :HD], q2, NT) + jnp.concatenate([add, add], axis=1)
                e_ref[rows, cols] = x
                top = jnp.maximum(top, jnp.max(fold(x), axis=0))
            top = jnp.max(top, axis=0, keepdims=True) * coef
            total = jnp.zeros((8, width), jnp.float32)
            weighted = jnp.zeros((8, width), jnp.float32)
            for k in range(half):
                rows = slice(k * local, (k + 1) * local)
                e = jnp.exp2(e_ref[rows, cols] * coef - top)
                d = dot(kv_refs[k][:, HD:], do2, NT)
                total = total + jnp.sum(fold(e), axis=0)
                weighted = weighted + jnp.sum(fold(e * d), axis=0)
                e_ref[rows, cols] = e
                d_ref[rows, cols] = d
            stat_ref[0:1, cols] = top
            stat_ref[1:2, cols] = jnp.sum(total, axis=0, keepdims=True)
            stat_ref[2:3, cols] = jnp.sum(weighted, axis=0, keepdims=True)
    stat_ref[3:8, :] = jnp.zeros((5, stat_ref.shape[1]), jnp.float32)


def gradients_kernel(half, local, *refs):
    e_ref, d_ref, mine_ref, other_ref, q_rows, do_rows = refs[:6]
    kv_refs = refs[6 : 6 + half]
    gq_ref, gq_other_ref, own_ref = refs[6 + half : 9 + half]
    part_refs = refs[9 + half : 8 + 2 * half]
    k_t, p_buf, ds_buf = refs[8 + 2 * half :]
    columns = e_ref.shape[1]
    heads = columns // (2 * local)
    side = columns // 2
    width = 2 * local

    for k in range(half):
        k_t[:, k * local : (k + 1) * local] = kv_refs[k][:, :HD].T
    for c in range(0, columns, width):
        cols = slice(c, c + width)
        across = slice((c + side) % columns, (c + side) % columns + width)
        top = jnp.maximum(mine_ref[0:1, cols], other_ref[0:1, across])
        factor = jnp.exp2(mine_ref[0:1, cols] - top)
        factor_other = jnp.exp2(other_ref[0:1, across] - top)
        total = mine_ref[1:2, cols] * factor + other_ref[1:2, across] * factor_other
        weighted = mine_ref[2:3, cols] * factor + other_ref[2:3, across] * factor_other
        inv = 1.0 / total
        delta = weighted * inv
        factor = factor * inv
        for k in range(half):
            rows = slice(k * local, (k + 1) * local)
            p = e_ref[rows, cols] * factor
            ds = p * (d_ref[rows, cols] - delta)
            p_buf[rows, cols] = p.astype(jnp.bfloat16)
            ds_buf[rows, cols] = ds.astype(jnp.bfloat16)

    gk = dot(ds_buf[...], q_rows[...]) * SCALE
    gv = dot(p_buf[...], do_rows[...])
    own_ref[:, :HD] = gk[:local]
    own_ref[:, HD:] = gv[:local]
    for k in range(1, half):
        rows = slice(k * local, (k + 1) * local)
        part_refs[k - 1][:, :HD] = gk[rows].astype(jnp.bfloat16)
        part_refs[k - 1][:, HD:] = gv[rows].astype(jnp.bfloat16)
    gq = dot(k_t[...], ds_buf[...]) * SCALE
    for h in range(heads):
        cols = slice(h * HD, (h + 1) * HD)
        gq_ref[:, cols] = gq[:, h * local : (h + 1) * local].T
        gq_other_ref[:, cols] = gq[:, side + h * local : side + (h + 1) * local].T


def attention(lengths, me, kv, q, do, q_other, do_other):
    half = len(kv)
    local, width = q.shape
    keys = half * local
    heads = width // HD
    columns = 2 * heads * local
    vm = pl.BlockSpec(memory_space=pltpu.VMEM)
    sm = pl.BlockSpec(memory_space=pltpu.SMEM)
    bf16, f32 = jnp.bfloat16, jnp.float32
    e, d, stat, q_rows, do_rows = pl.pallas_call(
        functools.partial(scores_kernel, half, local, lengths.shape[1]),
        out_shape=(
            jax.ShapeDtypeStruct((keys, columns), f32),
            jax.ShapeDtypeStruct((keys, columns), f32),
            jax.ShapeDtypeStruct((8, columns), f32),
            jax.ShapeDtypeStruct((columns, HD), bf16),
            jax.ShapeDtypeStruct((columns, HD), bf16),
        ),
        in_specs=[sm, sm] + [vm] * (half + 4),
        out_specs=(vm,) * 5,
        scratch_shapes=[pltpu.VMEM((2, keys, local), f32)],
        cost_estimate=pl.CostEstimate(flops=COST1, bytes_accessed=0, transcendentals=0),
        compiler_params=pltpu.CompilerParams(vmem_limit_bytes=keys * 44 * 1024),
    )(lengths, me, *kv, q, q_other, do, do_other)
    stat_other = swap(stat, "ctx", 1)
    return pl.pallas_call(
        functools.partial(gradients_kernel, half, local),
        out_shape=(
            jax.ShapeDtypeStruct((local, width), f32),
            jax.ShapeDtypeStruct((local, width), f32),
            jax.ShapeDtypeStruct((local, 2 * HD), f32),
        )
        + (jax.ShapeDtypeStruct((local, 2 * HD), bf16),) * (half - 1),
        in_specs=[vm] * (half + 6),
        out_specs=(vm,) * (half + 2),
        scratch_shapes=[
            pltpu.VMEM((HD, keys), bf16),
            pltpu.VMEM((keys, columns), bf16),
            pltpu.VMEM((keys, columns), bf16),
        ],
        cost_estimate=pl.CostEstimate(flops=COST2, bytes_accessed=0, transcendentals=0),
        compiler_params=pltpu.CompilerParams(vmem_limit_bytes=keys * 44 * 1024),
    )(e, d, stat, stat_other, q_rows, do_rows, *kv)


COST1 = 1_000_000_000
COST2 = 1_000_000_000


def on_device(inputs, queries, keys_values, out_grad, lengths):
    stripes = lax.axis_size("ctx")
    rows = lax.axis_size("dp")
    half = stripes // 2
    me = lax.axis_index("ctx")
    row = lax.axis_index("dp")
    x = inputs[0, 0]
    q = queries[0, 0]
    do = out_grad[0, 0]
    kv = keys_values[0, 0]
    local, features = x.shape
    part = features // (stripes * rows)

    kv_own = [kv] + [swap(kv, "ctx", 2 * k) for k in range(1, half)]
    q_other = swap(q, "ctx", 1)
    do_other = swap(do, "ctx", 1)

    x, q_other, do_other = lax.optimization_barrier((x, q_other, do_other))
    xb = x.reshape(local, stripes, rows, part)
    x_slabs = []
    for k in range(rows):
        slab = lax.dynamic_index_in_dim(xb, row ^ k, 2, keepdims=False)
        slab = slab.reshape(local, stripes * part)
        x_slabs.append(slab if k == 0 else swap(slab, "dp", k))

    gq, gq_other, own, *parts = attention(
        lengths, me.reshape(1).astype(jnp.int32), kv_own, q, do, q_other, do_other
    )
    parts, early = lax.optimization_barrier((parts, [x_slabs[k] for k in (3,)]))
    for k, slab in zip((3,), early):
        x_slabs[k] = slab

    terms = [swap(parts[k - 1], "ctx", 2 * k) for k in range(1, half)]
    gkv = own + sum(t.astype(jnp.float32) for t in terms)
    gkv = gkv.astype(jnp.bfloat16)
    gq = (gq + swap(gq_other, "ctx", 1)).astype(jnp.bfloat16)

    g_rows = [gkv] + [swap(gkv, "dp", k) for k in range(1, rows)]
    x_all = jnp.concatenate(x_slabs, axis=0)
    g_all = jnp.concatenate(g_rows, axis=0)
    w = dot(x_all, g_all, TN) * (1.0 / rows)
    w = w.reshape(half, 2, part, 2 * HD)
    core = me % 2
    w_own = lax.dynamic_index_in_dim(w, core, 1, keepdims=False)
    w_sib = lax.dynamic_index_in_dim(w, 1 - core, 1, keepdims=False)
    w_chip = w_own + swap(w_sib.astype(jnp.bfloat16), "ctx", 1).astype(jnp.float32)
    z = me // 2
    w_mine = lax.dynamic_index_in_dim(w_chip, z, 0, keepdims=False)
    for k in range(1, half):
        block = lax.dynamic_index_in_dim(w_chip, z ^ k, 0, keepdims=False)
        w_mine = w_mine + swap(block.astype(jnp.bfloat16), "ctx", 2 * k).astype(jnp.float32)

    low = w_mine.astype(jnp.bfloat16)
    low, gq = lax.optimization_barrier((low, gq))
    blocks = [low] + [swap(low, "dp", k) for k in range(1, rows)]
    bit = 1
    while bit < rows:
        flip = (row & bit) != 0
        blocks = [jnp.where(flip, blocks[j ^ bit], blocks[j]) for j in range(rows)]
        bit *= 2
    w_out = jnp.concatenate([b.astype(jnp.float32) for b in blocks], axis=0)
    return (
        gq.reshape(1, 1, local, -1),
        gkv.reshape(1, 1, local, 2 * HD),
        w_out,
    )


def solution(mesh):
    spec = P("dp", "ctx", None, None)
    return jax.shard_map(
        on_device,
        mesh=mesh,
        in_specs=(spec, spec, spec, spec, P("dp", None)),
        out_specs=(spec, spec, P("ctx", None)),
        check_vma=False,
    )
```

```python
import functools

import jax
import jax.numpy as jnp
from jax import lax
from jax.experimental import pallas as pl
from jax.experimental.pallas import tpu as pltpu
from jax.sharding import PartitionSpec as P

HD = 128
RESPONSES = 4
LOG2E = 1.4426950408889634
NEG = -1e30
SCALE = HD**-0.5

NT = (((1,), (1,)), ((), ()))
TN = (((0,), (0,)), ((), ()))


def dot(a, b, dims=(((1,), (0,)), ((), ()))):
    return lax.dot_general(a, b, dims, preferred_element_type=jnp.float32)


def swap(x, axis, mask):
    size = lax.axis_size(axis)
    return lax.ppermute(x, axis, [(i, i ^ mask) for i in range(size)])


def fold(x):
    return x.reshape(x.shape[0] // 8, 8, x.shape[1])


def mask_kernel(half, local, pieces, *refs):
    len_ref, me_ref, *ins = refs[:6]
    q_refs, do_refs = ins[:2], ins[2:]
    bias, q_rows, do_rows = refs[6:]
    stripes = 2 * half
    me = me_ref[0]
    heads = q_refs[0].shape[1] // HD
    per_group = RESPONSES + 1
    for b in range(2):
        for h in range(heads):
            rows = slice((b * heads + h) * local, (b * heads + h + 1) * local)
            q_rows[rows, :] = q_refs[b][:, h * HD : (h + 1) * HD]
            do_rows[rows, :] = do_refs[b][:, h * HD : (h + 1) * HD]

    row_pos = lax.broadcasted_iota(jnp.int32, (local, local), 0) * stripes
    for b in range(2):
        q_pos = lax.broadcasted_iota(jnp.int32, (1, local), 1) * stripes + (me ^ b)
        own_start = jnp.zeros((1, local), jnp.int32)
        prompt_start = jnp.zeros((1, local), jnp.int32)
        prompt_end = jnp.zeros((1, local), jnp.int32)
        start = jnp.int32(0)
        for k in range(pieces):
            length = len_ref[0, k]
            inside = q_pos >= start
            own_start = jnp.where(inside, start, own_start)
            if k % per_group == 0:
                prompt_start = jnp.where(inside, start, prompt_start)
                prompt_end = jnp.where(inside, start + length, prompt_end)
            start = start + length
        prompt_end = jnp.minimum(prompt_end, q_pos + 1)
        for k in range(half):
            k_pos = row_pos + (me ^ (2 * k))
            ok = ((k_pos >= own_start) & (k_pos <= q_pos)) | (
                (k_pos >= prompt_start) & (k_pos < prompt_end)
            )
            bias[b, k * local : (k + 1) * local, :] = jnp.where(ok, 0.0, NEG)


def scores_kernel(half, local, *refs):
    kv_refs = refs[:half]
    bias, q_rows, do_rows, e_ref, d_ref, stat_ref = refs[half:]
    heads = q_rows.shape[0] // (2 * local)
    coef = SCALE * LOG2E
    width = 2 * local
    for b in range(2):
        for pair in range(heads // 2):
            cols = slice((b * heads + 2 * pair) * local, (b * heads + 2 * pair + 2) * local)
            q2 = q_rows[cols, :]
            do2 = do_rows[cols, :]
            top = jnp.full((8, width), NEG, jnp.float32)
            for k in range(half):
                rows = slice(k * local, (k + 1) * local)
                add = bias[b, rows, :]
                x = dot(kv_refs[k][:, :HD], q2, NT) + jnp.concatenate([add, add], axis=1)
                e_ref[rows, cols] = x
                top = jnp.maximum(top, jnp.max(fold(x), axis=0))
            top = jnp.max(top, axis=0, keepdims=True) * coef
            total = jnp.zeros((8, width), jnp.float32)
            weighted = jnp.zeros((8, width), jnp.float32)
            for k in range(half):
                rows = slice(k * local, (k + 1) * local)
                e = jnp.exp2(e_ref[rows, cols] * coef - top)
                d = dot(kv_refs[k][:, HD:], do2, NT)
                total = total + jnp.sum(fold(e), axis=0)
                weighted = weighted + jnp.sum(fold(e * d), axis=0)
                e_ref[rows, cols] = e
                d_ref[rows, cols] = d
            stat_ref[0:1, cols] = top
            stat_ref[1:2, cols] = jnp.sum(total, axis=0, keepdims=True)
            stat_ref[2:3, cols] = jnp.sum(weighted, axis=0, keepdims=True)
    stat_ref[3:8, :] = jnp.zeros((5, stat_ref.shape[1]), jnp.float32)


def gradients_kernel(half, local, *refs):
    e_ref, d_ref, mine_ref, other_ref, q_rows, do_rows = refs[:6]
    kv_refs = refs[6 : 6 + half]
    gq_ref, gq_other_ref, own_ref = refs[6 + half : 9 + half]
    part_refs = refs[9 + half : 8 + 2 * half]
    k_t, p_buf, ds_buf = refs[8 + 2 * half :]
    columns = e_ref.shape[1]
    heads = columns // (2 * local)
    side = columns // 2
    width = 2 * local

    for k in range(half):
        k_t[:, k * local : (k + 1) * local] = kv_refs[k][:, :HD].T
    for c in range(0, columns, width):
        cols = slice(c, c + width)
        across = slice((c + side) % columns, (c + side) % columns + width)
        top = jnp.maximum(mine_ref[0:1, cols], other_ref[0:1, across])
        factor = jnp.exp2(mine_ref[0:1, cols] - top)
        factor_other = jnp.exp2(other_ref[0:1, across] - top)
        total = mine_ref[1:2, cols] * factor + other_ref[1:2, across] * factor_other
        weighted = mine_ref[2:3, cols] * factor + other_ref[2:3, across] * factor_other
        inv = 1.0 / total
        delta = weighted * inv
        factor = factor * inv
        for k in range(half):
            rows = slice(k * local, (k + 1) * local)
            p = e_ref[rows, cols] * factor
            ds = p * (d_ref[rows, cols] - delta)
            p_buf[rows, cols] = p.astype(jnp.bfloat16)
            ds_buf[rows, cols] = ds.astype(jnp.bfloat16)

    gk = dot(ds_buf[...], q_rows[...]) * SCALE
    gv = dot(p_buf[...], do_rows[...])
    own_ref[:, :HD] = gk[:local]
    own_ref[:, HD:] = gv[:local]
    for k in range(1, half):
        rows = slice(k * local, (k + 1) * local)
        part_refs[k - 1][:, :HD] = gk[rows].astype(jnp.bfloat16)
        part_refs[k - 1][:, HD:] = gv[rows].astype(jnp.bfloat16)
    gq = dot(k_t[...], ds_buf[...]) * SCALE
    for h in range(heads):
        cols = slice(h * HD, (h + 1) * HD)
        gq_ref[:, cols] = gq[:, h * local : (h + 1) * local].T
        gq_other_ref[:, cols] = gq[:, side + h * local : side + (h + 1) * local].T


def attention(lengths, me, kv, q, do, q_other, do_other):
    half = len(kv)
    local, width = q.shape
    keys = half * local
    heads = width // HD
    columns = 2 * heads * local
    vm = pl.BlockSpec(memory_space=pltpu.VMEM)
    sm = pl.BlockSpec(memory_space=pltpu.SMEM)
    bf16, f32 = jnp.bfloat16, jnp.float32
    bias, q_rows, do_rows = pl.pallas_call(
        functools.partial(mask_kernel, half, local, lengths.shape[1]),
        out_shape=(
            jax.ShapeDtypeStruct((2, keys, local), f32),
            jax.ShapeDtypeStruct((columns, HD), bf16),
            jax.ShapeDtypeStruct((columns, HD), bf16),
        ),
        in_specs=[sm, sm] + [vm] * 4,
        out_specs=(vm,) * 3,
        cost_estimate=pl.CostEstimate(flops=COST0, bytes_accessed=0, transcendentals=0),
        compiler_params=pltpu.CompilerParams(vmem_limit_bytes=keys * 20 * 1024),
    )(lengths, me, q, q_other, do, do_other)
    e, d, stat = pl.pallas_call(
        functools.partial(scores_kernel, half, local),
        out_shape=(
            jax.ShapeDtypeStruct((keys, columns), f32),
            jax.ShapeDtypeStruct((keys, columns), f32),
            jax.ShapeDtypeStruct((8, columns), f32),
        ),
        in_specs=[vm] * (half + 3),
        out_specs=(vm,) * 3,
        cost_estimate=pl.CostEstimate(flops=COST1, bytes_accessed=0, transcendentals=0),
        compiler_params=pltpu.CompilerParams(vmem_limit_bytes=keys * 44 * 1024),
    )(*kv, bias, q_rows, do_rows)
    stat_other = swap(stat, "ctx", 1)
    return pl.pallas_call(
        functools.partial(gradients_kernel, half, local),
        out_shape=(
            jax.ShapeDtypeStruct((local, width), f32),
            jax.ShapeDtypeStruct((local, width), f32),
            jax.ShapeDtypeStruct((local, 2 * HD), f32),
        )
        + (jax.ShapeDtypeStruct((local, 2 * HD), bf16),) * (half - 1),
        in_specs=[vm] * (half + 6),
        out_specs=(vm,) * (half + 2),
        scratch_shapes=[
            pltpu.VMEM((HD, keys), bf16),
            pltpu.VMEM((keys, columns), bf16),
            pltpu.VMEM((keys, columns), bf16),
        ],
        cost_estimate=pl.CostEstimate(flops=COST2, bytes_accessed=0, transcendentals=0),
        compiler_params=pltpu.CompilerParams(vmem_limit_bytes=keys * 44 * 1024),
    )(e, d, stat, stat_other, q_rows, do_rows, *kv)


COST0 = 1_000_000_000
COST1 = 2_000_000_000
COST2 = 2_000_000_000


def on_device(inputs, queries, keys_values, out_grad, lengths):
    stripes = lax.axis_size("ctx")
    rows = lax.axis_size("dp")
    half = stripes // 2
    me = lax.axis_index("ctx")
    row = lax.axis_index("dp")
    x = inputs[0, 0]
    q = queries[0, 0]
    do = out_grad[0, 0]
    kv = keys_values[0, 0]
    local, features = x.shape
    part = features // (stripes * rows)

    kv_own = [kv] + [swap(kv, "ctx", 2 * k) for k in range(1, half)]
    q_other = swap(q, "ctx", 1)
    do_other = swap(do, "ctx", 1)

    x, q_other, do_other = lax.optimization_barrier((x, q_other, do_other))
    xb = x.reshape(local, stripes, rows, part)
    x_slabs = []
    for k in range(rows):
        slab = lax.dynamic_index_in_dim(xb, row ^ k, 2, keepdims=False)
        slab = slab.reshape(local, stripes * part)
        x_slabs.append(slab if k == 0 else swap(slab, "dp", k))

    gq, gq_other, own, *parts = attention(
        lengths, me.reshape(1).astype(jnp.int32), kv_own, q, do, q_other, do_other
    )
    parts, early = lax.optimization_barrier((parts, [x_slabs[k] for k in (3,)]))
    for k, slab in zip((3,), early):
        x_slabs[k] = slab

    terms = [swap(parts[k - 1], "ctx", 2 * k) for k in range(1, half)]
    gkv = own + sum(t.astype(jnp.float32) for t in terms)
    gkv = gkv.astype(jnp.bfloat16)
    gq = (gq + swap(gq_other, "ctx", 1)).astype(jnp.bfloat16)

    g_rows = [gkv] + [swap(gkv, "dp", k) for k in range(1, rows)]
    x_all = jnp.concatenate(x_slabs, axis=0)
    g_all = jnp.concatenate(g_rows, axis=0)
    w = dot(x_all, g_all, TN) * (1.0 / rows)
    w = w.reshape(half, 2, part, 2 * HD)
    core = me % 2
    w_own = lax.dynamic_index_in_dim(w, core, 1, keepdims=False)
    w_sib = lax.dynamic_index_in_dim(w, 1 - core, 1, keepdims=False)
    w_chip = w_own + swap(w_sib.astype(jnp.bfloat16), "ctx", 1).astype(jnp.float32)
    z = me // 2
    w_mine = lax.dynamic_index_in_dim(w_chip, z, 0, keepdims=False)
    for k in range(1, half):
        block = lax.dynamic_index_in_dim(w_chip, z ^ k, 0, keepdims=False)
        w_mine = w_mine + swap(block.astype(jnp.bfloat16), "ctx", 2 * k).astype(jnp.float32)

    low = w_mine.astype(jnp.bfloat16)
    low, gq = lax.optimization_barrier((low, gq))
    blocks = [low] + [swap(low, "dp", k) for k in range(1, rows)]
    bit = 1
    while bit < rows:
        flip = (row & bit) != 0
        blocks = [jnp.where(flip, blocks[j ^ bit], blocks[j]) for j in range(rows)]
        bit *= 2
    w_out = jnp.concatenate([b.astype(jnp.float32) for b in blocks], axis=0)
    return (
        gq.reshape(1, 1, local, -1),
        gkv.reshape(1, 1, local, 2 * HD),
        w_out,
    )


def solution(mesh):
    spec = P("dp", "ctx", None, None)
    return jax.shard_map(
        on_device,
        mesh=mesh,
        in_specs=(spec, spec, spec, spec, P("dp", None)),
        out_specs=(spec, spec, P("ctx", None)),
        check_vma=False,
    )
```

```python
import functools

import jax
import jax.numpy as jnp
from jax import lax
from jax.experimental import pallas as pl
from jax.experimental.pallas import tpu as pltpu
from jax.sharding import PartitionSpec as P

HD = 128
RESPONSES = 4
LOG2E = 1.4426950408889634
NEG = -1e30
SCALE = HD**-0.5

NT = (((1,), (1,)), ((), ()))
TN = (((0,), (0,)), ((), ()))


def dot(a, b, dims=(((1,), (0,)), ((), ()))):
    return lax.dot_general(a, b, dims, preferred_element_type=jnp.float32)


def swap(x, axis, mask):
    size = lax.axis_size(axis)
    return lax.ppermute(x, axis, [(i, i ^ mask) for i in range(size)])


def fold(x):
    return x.reshape(x.shape[0] // 8, 8, x.shape[1])


def mask_kernel(half, local, pieces, *refs):
    len_ref, me_ref, *ins = refs[:6]
    q_refs, do_refs = ins[:2], ins[2:]
    bias, q_rows, do_rows = refs[6:]
    stripes = 2 * half
    me = me_ref[0]
    heads = q_refs[0].shape[1] // HD
    per_group = RESPONSES + 1
    for b in range(2):
        for h in range(heads):
            rows = slice((b * heads + h) * local, (b * heads + h + 1) * local)
            q_rows[rows, :] = q_refs[b][:, h * HD : (h + 1) * HD]
            do_rows[rows, :] = do_refs[b][:, h * HD : (h + 1) * HD]

    row_pos = lax.broadcasted_iota(jnp.int32, (local, local), 0) * stripes
    for b in range(2):
        q_pos = lax.broadcasted_iota(jnp.int32, (1, local), 1) * stripes + (me ^ b)
        own_start = jnp.zeros((1, local), jnp.int32)
        prompt_start = jnp.zeros((1, local), jnp.int32)
        prompt_end = jnp.zeros((1, local), jnp.int32)
        start = jnp.int32(0)
        for k in range(pieces):
            length = len_ref[0, k]
            inside = q_pos >= start
            own_start = jnp.where(inside, start, own_start)
            if k % per_group == 0:
                prompt_start = jnp.where(inside, start, prompt_start)
                prompt_end = jnp.where(inside, start + length, prompt_end)
            start = start + length
        prompt_end = jnp.minimum(prompt_end, q_pos + 1)
        for k in range(half):
            k_pos = row_pos + (me ^ (2 * k))
            ok = ((k_pos >= own_start) & (k_pos <= q_pos)) | (
                (k_pos >= prompt_start) & (k_pos < prompt_end)
            )
            bias[b, k * local : (k + 1) * local, :] = jnp.where(ok, 0.0, NEG)


def scores_kernel(half, local, *refs):
    kv_refs = refs[:half]
    bias, q_rows, do_rows, e_ref, d_ref, stat_ref = refs[half:]
    heads = q_rows.shape[0] // (2 * local)
    coef = SCALE * LOG2E
    width = 4 * local
    for b in range(2):
        for group in range(heads // 4):
            first = b * heads + 4 * group
            cols = slice(first * local, (first + 4) * local)
            q2 = q_rows[cols, :]
            do2 = do_rows[cols, :]
            top = jnp.full((8, width), NEG, jnp.float32)
            for k in range(half):
                rows = slice(k * local, (k + 1) * local)
                add = bias[b, rows, :]
                x = dot(kv_refs[k][:, :HD], q2, NT) + jnp.concatenate([add] * 4, axis=1)
                e_ref[rows, cols] = x
                top = jnp.maximum(top, jnp.max(fold(x), axis=0))
            top = jnp.max(top, axis=0, keepdims=True) * coef
            total = jnp.zeros((8, width), jnp.float32)
            weighted = jnp.zeros((8, width), jnp.float32)
            for k in range(half):
                rows = slice(k * local, (k + 1) * local)
                e = jnp.exp2(e_ref[rows, cols] * coef - top)
                d = dot(kv_refs[k][:, HD:], do2, NT)
                total = total + jnp.sum(fold(e), axis=0)
                weighted = weighted + jnp.sum(fold(e * d), axis=0)
                e_ref[rows, cols] = e
                d_ref[rows, cols] = d
            stat_ref[0:1, cols] = top
            stat_ref[1:2, cols] = jnp.sum(total, axis=0, keepdims=True)
            stat_ref[2:3, cols] = jnp.sum(weighted, axis=0, keepdims=True)
    stat_ref[3:8, :] = jnp.zeros((5, stat_ref.shape[1]), jnp.float32)


def gradients_kernel(half, local, *refs):
    e_ref, d_ref, mine_ref, other_ref, q_rows, do_rows = refs[:6]
    kv_refs = refs[6 : 6 + half]
    gq_ref, gq_other_ref, own_ref = refs[6 + half : 9 + half]
    part_refs = refs[9 + half : 8 + 2 * half]
    k_t, p_buf, ds_buf = refs[8 + 2 * half :]
    columns = e_ref.shape[1]
    heads = columns // (2 * local)
    side = columns // 2
    width = 2 * local

    for k in range(half):
        k_t[:, k * local : (k + 1) * local] = kv_refs[k][:, :HD].T
    for c in range(0, columns, width):
        cols = slice(c, c + width)
        across = slice((c + side) % columns, (c + side) % columns + width)
        top = jnp.maximum(mine_ref[0:1, cols], other_ref[0:1, across])
        factor = jnp.exp2(mine_ref[0:1, cols] - top)
        factor_other = jnp.exp2(other_ref[0:1, across] - top)
        total = mine_ref[1:2, cols] * factor + other_ref[1:2, across] * factor_other
        weighted = mine_ref[2:3, cols] * factor + other_ref[2:3, across] * factor_other
        inv = 1.0 / total
        delta = weighted * inv
        factor = factor * inv
        for k in range(half):
            rows = slice(k * local, (k + 1) * local)
            p = e_ref[rows, cols] * factor
            ds = p * (d_ref[rows, cols] - delta)
            p_buf[rows, cols] = p.astype(jnp.bfloat16)
            ds_buf[rows, cols] = ds.astype(jnp.bfloat16)

    gk = dot(ds_buf[...], q_rows[...]) * SCALE
    gv = dot(p_buf[...], do_rows[...])
    own_ref[:, :HD] = gk[:local]
    own_ref[:, HD:] = gv[:local]
    for k in range(1, half):
        rows = slice(k * local, (k + 1) * local)
        part_refs[k - 1][:, :HD] = gk[rows].astype(jnp.bfloat16)
        part_refs[k - 1][:, HD:] = gv[rows].astype(jnp.bfloat16)
    gq = dot(k_t[...], ds_buf[...]) * SCALE
    for h in range(heads):
        cols = slice(h * HD, (h + 1) * HD)
        gq_ref[:, cols] = gq[:, h * local : (h + 1) * local].T
        gq_other_ref[:, cols] = gq[:, side + h * local : side + (h + 1) * local].T


def attention(lengths, me, kv, q, do, q_other, do_other):
    half = len(kv)
    local, width = q.shape
    keys = half * local
    heads = width // HD
    columns = 2 * heads * local
    vm = pl.BlockSpec(memory_space=pltpu.VMEM)
    sm = pl.BlockSpec(memory_space=pltpu.SMEM)
    bf16, f32 = jnp.bfloat16, jnp.float32
    bias, q_rows, do_rows = pl.pallas_call(
        functools.partial(mask_kernel, half, local, lengths.shape[1]),
        out_shape=(
            jax.ShapeDtypeStruct((2, keys, local), f32),
            jax.ShapeDtypeStruct((columns, HD), bf16),
            jax.ShapeDtypeStruct((columns, HD), bf16),
        ),
        in_specs=[sm, sm] + [vm] * 4,
        out_specs=(vm,) * 3,
        cost_estimate=pl.CostEstimate(flops=COST0, bytes_accessed=0, transcendentals=0),
        compiler_params=pltpu.CompilerParams(vmem_limit_bytes=keys * 20 * 1024),
    )(lengths, me, q, q_other, do, do_other)
    e, d, stat = pl.pallas_call(
        functools.partial(scores_kernel, half, local),
        out_shape=(
            jax.ShapeDtypeStruct((keys, columns), f32),
            jax.ShapeDtypeStruct((keys, columns), f32),
            jax.ShapeDtypeStruct((8, columns), f32),
        ),
        in_specs=[vm] * (half + 3),
        out_specs=(vm,) * 3,
        cost_estimate=pl.CostEstimate(flops=COST1, bytes_accessed=0, transcendentals=0),
        compiler_params=pltpu.CompilerParams(vmem_limit_bytes=keys * 44 * 1024),
    )(*kv, bias, q_rows, do_rows)
    stat_other = swap(stat, "ctx", 1)
    return pl.pallas_call(
        functools.partial(gradients_kernel, half, local),
        out_shape=(
            jax.ShapeDtypeStruct((local, width), f32),
            jax.ShapeDtypeStruct((local, width), f32),
            jax.ShapeDtypeStruct((local, 2 * HD), f32),
        )
        + (jax.ShapeDtypeStruct((local, 2 * HD), bf16),) * (half - 1),
        in_specs=[vm] * (half + 6),
        out_specs=(vm,) * (half + 2),
        scratch_shapes=[
            pltpu.VMEM((HD, keys), bf16),
            pltpu.VMEM((keys, columns), bf16),
            pltpu.VMEM((keys, columns), bf16),
        ],
        cost_estimate=pl.CostEstimate(flops=COST2, bytes_accessed=0, transcendentals=0),
        compiler_params=pltpu.CompilerParams(vmem_limit_bytes=keys * 44 * 1024),
    )(e, d, stat, stat_other, q_rows, do_rows, *kv)


COST0 = 1_000_000_000
COST1 = 2_000_000_000
COST2 = 2_000_000_000


def on_device(inputs, queries, keys_values, out_grad, lengths):
    stripes = lax.axis_size("ctx")
    rows = lax.axis_size("dp")
    half = stripes // 2
    me = lax.axis_index("ctx")
    row = lax.axis_index("dp")
    x = inputs[0, 0]
    q = queries[0, 0]
    do = out_grad[0, 0]
    kv = keys_values[0, 0]
    local, features = x.shape
    part = features // (stripes * rows)

    kv_own = [kv] + [swap(kv, "ctx", 2 * k) for k in range(1, half)]
    q_other = swap(q, "ctx", 1)
    do_other = swap(do, "ctx", 1)

    x, q_other, do_other = lax.optimization_barrier((x, q_other, do_other))
    xb = x.reshape(local, stripes, rows, part)
    x_slabs = []
    for k in range(rows):
        slab = lax.dynamic_index_in_dim(xb, row ^ k, 2, keepdims=False)
        slab = slab.reshape(local, stripes * part)
        x_slabs.append(slab if k == 0 else swap(slab, "dp", k))

    gq, gq_other, own, *parts = attention(
        lengths, me.reshape(1).astype(jnp.int32), kv_own, q, do, q_other, do_other
    )
    parts, early = lax.optimization_barrier((parts, [x_slabs[k] for k in (3,)]))
    for k, slab in zip((3,), early):
        x_slabs[k] = slab

    terms = [swap(parts[k - 1], "ctx", 2 * k) for k in reversed(range(1, half))]
    gkv = own + sum(t.astype(jnp.float32) for t in terms)
    gkv = gkv.astype(jnp.bfloat16)
    gq = (gq + swap(gq_other, "ctx", 1)).astype(jnp.bfloat16)

    g_rows = [gkv] + [swap(gkv, "dp", k) for k in range(1, rows)]
    x_all = jnp.concatenate(x_slabs, axis=0)
    g_all = jnp.concatenate(g_rows, axis=0)
    w = dot(x_all, g_all, TN) * (1.0 / rows)
    w = w.reshape(half, 2, part, 2 * HD)
    core = me % 2
    w_own = lax.dynamic_index_in_dim(w, core, 1, keepdims=False)
    w_sib = lax.dynamic_index_in_dim(w, 1 - core, 1, keepdims=False)
    w_chip = w_own + swap(w_sib.astype(jnp.bfloat16), "ctx", 1).astype(jnp.float32)
    z = me // 2
    w_mine = lax.dynamic_index_in_dim(w_chip, z, 0, keepdims=False)
    for k in reversed(range(1, half)):
        block = lax.dynamic_index_in_dim(w_chip, z ^ k, 0, keepdims=False)
        w_mine = w_mine + swap(block.astype(jnp.bfloat16), "ctx", 2 * k).astype(jnp.float32)

    low = w_mine.astype(jnp.bfloat16)
    low, gq = lax.optimization_barrier((low, gq))
    blocks = [low] + [swap(low, "dp", k) for k in range(1, rows)]
    bit = 1
    while bit < rows:
        flip = (row & bit) != 0
        blocks = [jnp.where(flip, blocks[j ^ bit], blocks[j]) for j in range(rows)]
        bit *= 2
    w_out = jnp.concatenate([b.astype(jnp.float32) for b in blocks], axis=0)
    return (
        gq.reshape(1, 1, local, -1),
        gkv.reshape(1, 1, local, 2 * HD),
        w_out,
    )


def solution(mesh):
    spec = P("dp", "ctx", None, None)
    return jax.shard_map(
        on_device,
        mesh=mesh,
        in_specs=(spec, spec, spec, spec, P("dp", None)),
        out_specs=(spec, spec, P("ctx", None)),
        check_vma=False,
    )
```

```python
import functools

import jax
import jax.numpy as jnp
from jax import lax
from jax.experimental import pallas as pl
from jax.experimental.pallas import tpu as pltpu
from jax.sharding import PartitionSpec as P

HD = 128
RESPONSES = 4
LOG2E = 1.4426950408889634
NEG = -1e30
SCALE = HD**-0.5

NT = (((1,), (1,)), ((), ()))
TN = (((0,), (0,)), ((), ()))


def dot(a, b, dims=(((1,), (0,)), ((), ()))):
    return lax.dot_general(a, b, dims, preferred_element_type=jnp.float32)


def swap(x, axis, mask):
    size = lax.axis_size(axis)
    return lax.ppermute(x, axis, [(i, i ^ mask) for i in range(size)])


def fold(x):
    return x.reshape(x.shape[0] // 8, 8, x.shape[1])


def mask_kernel(half, local, pieces, *refs):
    len_ref, me_ref, *ins = refs[:6]
    q_refs, do_refs = ins[:2], ins[2:]
    bias, q_rows, do_rows = refs[6:]
    stripes = 2 * half
    me = me_ref[0]
    heads = q_refs[0].shape[1] // HD
    per_group = RESPONSES + 1
    for b in range(2):
        for h in range(heads):
            rows = slice((b * heads + h) * local, (b * heads + h + 1) * local)
            q_rows[rows, :] = q_refs[b][:, h * HD : (h + 1) * HD]
            do_rows[rows, :] = do_refs[b][:, h * HD : (h + 1) * HD]

    row_pos = lax.broadcasted_iota(jnp.int32, (local, local), 0) * stripes
    for b in range(2):
        q_pos = lax.broadcasted_iota(jnp.int32, (1, local), 1) * stripes + (me ^ b)
        own_start = jnp.zeros((1, local), jnp.int32)
        prompt_start = jnp.zeros((1, local), jnp.int32)
        prompt_end = jnp.zeros((1, local), jnp.int32)
        start = jnp.int32(0)
        for k in range(pieces):
            length = len_ref[0, k]
            inside = q_pos >= start
            own_start = jnp.where(inside, start, own_start)
            if k % per_group == 0:
                prompt_start = jnp.where(inside, start, prompt_start)
                prompt_end = jnp.where(inside, start + length, prompt_end)
            start = start + length
        prompt_end = jnp.minimum(prompt_end, q_pos + 1)
        for k in range(half):
            k_pos = row_pos + (me ^ (2 * k))
            ok = ((k_pos >= own_start) & (k_pos <= q_pos)) | (
                (k_pos >= prompt_start) & (k_pos < prompt_end)
            )
            bias[b, k * local : (k + 1) * local, :] = jnp.where(ok, 0.0, NEG)


def scores_kernel(half, local, *refs):
    kv_refs = refs[:half]
    bias, q_rows, do_rows, e_ref, d_ref, stat_ref = refs[half:]
    heads = q_rows.shape[0] // (2 * local)
    coef = SCALE * LOG2E
    width = 8 * local
    for b in range(2):
        for group in range(heads // 8):
            first = b * heads + 8 * group
            cols = slice(first * local, (first + 8) * local)
            q2 = q_rows[cols, :]
            do2 = do_rows[cols, :]
            top = jnp.full((8, width), NEG, jnp.float32)
            for k in range(half):
                rows = slice(k * local, (k + 1) * local)
                add = bias[b, rows, :]
                x = dot(kv_refs[k][:, :HD], q2, NT) + jnp.concatenate([add] * 8, axis=1)
                e_ref[rows, cols] = x
                top = jnp.maximum(top, jnp.max(fold(x), axis=0))
            top = jnp.max(top, axis=0, keepdims=True) * coef
            total = jnp.zeros((8, width), jnp.float32)
            weighted = jnp.zeros((8, width), jnp.float32)
            for k in range(half):
                rows = slice(k * local, (k + 1) * local)
                e = jnp.exp2(e_ref[rows, cols] * coef - top)
                d = dot(kv_refs[k][:, HD:], do2, NT)
                total = total + jnp.sum(fold(e), axis=0)
                weighted = weighted + jnp.sum(fold(e * d), axis=0)
                e_ref[rows, cols] = e
                d_ref[rows, cols] = d
            stat_ref[0:1, cols] = top
            stat_ref[1:2, cols] = jnp.sum(total, axis=0, keepdims=True)
            stat_ref[2:3, cols] = jnp.sum(weighted, axis=0, keepdims=True)
    stat_ref[3:8, :] = jnp.zeros((5, stat_ref.shape[1]), jnp.float32)


def gradients_kernel(half, local, *refs):
    e_ref, d_ref, mine_ref, other_ref, q_rows, do_rows = refs[:6]
    kv_refs = refs[6 : 6 + half]
    gq_ref, gq_other_ref, own_ref = refs[6 + half : 9 + half]
    part_refs = refs[9 + half : 8 + 2 * half]
    k_t, p_buf, ds_buf = refs[8 + 2 * half :]
    columns = e_ref.shape[1]
    heads = columns // (2 * local)
    side = columns // 2
    width = 4 * local

    for k in range(half):
        k_t[:, k * local : (k + 1) * local] = kv_refs[k][:, :HD].T
    for c in range(0, columns, width):
        cols = slice(c, c + width)
        across = slice((c + side) % columns, (c + side) % columns + width)
        top = jnp.maximum(mine_ref[0:1, cols], other_ref[0:1, across])
        factor = jnp.exp2(mine_ref[0:1, cols] - top)
        factor_other = jnp.exp2(other_ref[0:1, across] - top)
        total = mine_ref[1:2, cols] * factor + other_ref[1:2, across] * factor_other
        weighted = mine_ref[2:3, cols] * factor + other_ref[2:3, across] * factor_other
        inv = 1.0 / total
        delta = weighted * inv
        factor = factor * inv
        for k in range(half):
            rows = slice(k * local, (k + 1) * local)
            p = e_ref[rows, cols] * factor
            ds = p * (d_ref[rows, cols] - delta)
            p_buf[rows, cols] = p.astype(jnp.bfloat16)
            ds_buf[rows, cols] = ds.astype(jnp.bfloat16)

    gk = dot(ds_buf[...], q_rows[...]) * SCALE
    gv = dot(p_buf[...], do_rows[...])
    own_ref[:, :HD] = gk[:local]
    own_ref[:, HD:] = gv[:local]
    for k in range(1, half):
        rows = slice(k * local, (k + 1) * local)
        part_refs[k - 1][:, :HD] = gk[rows].astype(jnp.bfloat16)
        part_refs[k - 1][:, HD:] = gv[rows].astype(jnp.bfloat16)
    gq = dot(k_t[...], ds_buf[...]) * SCALE
    for h in range(heads):
        cols = slice(h * HD, (h + 1) * HD)
        gq_ref[:, cols] = gq[:, h * local : (h + 1) * local].T
        gq_other_ref[:, cols] = gq[:, side + h * local : side + (h + 1) * local].T


def attention(lengths, me, kv, q, do, q_other, do_other):
    half = len(kv)
    local, width = q.shape
    keys = half * local
    heads = width // HD
    columns = 2 * heads * local
    vm = pl.BlockSpec(memory_space=pltpu.VMEM)
    sm = pl.BlockSpec(memory_space=pltpu.SMEM)
    bf16, f32 = jnp.bfloat16, jnp.float32
    bias, q_rows, do_rows = pl.pallas_call(
        functools.partial(mask_kernel, half, local, lengths.shape[1]),
        out_shape=(
            jax.ShapeDtypeStruct((2, keys, local), f32),
            jax.ShapeDtypeStruct((columns, HD), bf16),
            jax.ShapeDtypeStruct((columns, HD), bf16),
        ),
        in_specs=[sm, sm] + [vm] * 4,
        out_specs=(vm,) * 3,
        cost_estimate=pl.CostEstimate(flops=COST0, bytes_accessed=0, transcendentals=0),
        compiler_params=pltpu.CompilerParams(vmem_limit_bytes=keys * 20 * 1024),
    )(lengths, me, q, q_other, do, do_other)
    e, d, stat = pl.pallas_call(
        functools.partial(scores_kernel, half, local),
        out_shape=(
            jax.ShapeDtypeStruct((keys, columns), f32),
            jax.ShapeDtypeStruct((keys, columns), f32),
            jax.ShapeDtypeStruct((8, columns), f32),
        ),
        in_specs=[vm] * (half + 3),
        out_specs=(vm,) * 3,
        cost_estimate=pl.CostEstimate(flops=COST1, bytes_accessed=0, transcendentals=0),
        compiler_params=pltpu.CompilerParams(vmem_limit_bytes=keys * 44 * 1024),
    )(*kv, bias, q_rows, do_rows)
    stat_other = swap(stat, "ctx", 1)
    return pl.pallas_call(
        functools.partial(gradients_kernel, half, local),
        out_shape=(
            jax.ShapeDtypeStruct((local, width), f32),
            jax.ShapeDtypeStruct((local, width), f32),
            jax.ShapeDtypeStruct((local, 2 * HD), f32),
        )
        + (jax.ShapeDtypeStruct((local, 2 * HD), bf16),) * (half - 1),
        in_specs=[vm] * (half + 6),
        out_specs=(vm,) * (half + 2),
        scratch_shapes=[
            pltpu.VMEM((HD, keys), bf16),
            pltpu.VMEM((keys, columns), bf16),
            pltpu.VMEM((keys, columns), bf16),
        ],
        cost_estimate=pl.CostEstimate(flops=COST2, bytes_accessed=0, transcendentals=0),
        compiler_params=pltpu.CompilerParams(vmem_limit_bytes=keys * 44 * 1024),
    )(e, d, stat, stat_other, q_rows, do_rows, *kv)


COST0 = 1_000_000_000
COST1 = 2_000_000_000
COST2 = 2_000_000_000


def on_device(inputs, queries, keys_values, out_grad, lengths):
    stripes = lax.axis_size("ctx")
    rows = lax.axis_size("dp")
    half = stripes // 2
    me = lax.axis_index("ctx")
    row = lax.axis_index("dp")
    x = inputs[0, 0]
    q = queries[0, 0]
    do = out_grad[0, 0]
    kv = keys_values[0, 0]
    local, features = x.shape
    part = features // (stripes * rows)

    kv_own = [kv] + [swap(kv, "ctx", 2 * k) for k in range(1, half)]
    q_other = swap(q, "ctx", 1)
    do_other = swap(do, "ctx", 1)

    x, q_other, do_other = lax.optimization_barrier((x, q_other, do_other))
    xb = x.reshape(local, stripes, rows, part)
    x_slabs = []
    for k in range(rows):
        slab = lax.dynamic_index_in_dim(xb, row ^ k, 2, keepdims=False)
        slab = slab.reshape(local, stripes * part)
        x_slabs.append(slab if k == 0 else swap(slab, "dp", k))

    gq, gq_other, own, *parts = attention(
        lengths, me.reshape(1).astype(jnp.int32), kv_own, q, do, q_other, do_other
    )
    parts, early = lax.optimization_barrier((parts, [x_slabs[k] for k in (3,)]))
    for k, slab in zip((3,), early):
        x_slabs[k] = slab

    terms = [swap(parts[k - 1], "ctx", 2 * k) for k in reversed(range(1, half))]
    gkv = own + sum(t.astype(jnp.float32) for t in terms)
    gkv = gkv.astype(jnp.bfloat16)
    gq = (gq + swap(gq_other, "ctx", 1)).astype(jnp.bfloat16)

    g_rows = [gkv] + [swap(gkv, "dp", k) for k in range(1, rows)]
    x_all = jnp.concatenate(x_slabs, axis=0)
    g_all = jnp.concatenate(g_rows, axis=0)
    w = dot(x_all, g_all, TN) * (1.0 / rows)
    w = w.reshape(half, 2, part, 2 * HD)
    core = me % 2
    w_own = lax.dynamic_index_in_dim(w, core, 1, keepdims=False)
    w_sib = lax.dynamic_index_in_dim(w, 1 - core, 1, keepdims=False)
    w_chip = w_own + swap(w_sib.astype(jnp.bfloat16), "ctx", 1).astype(jnp.float32)
    z = me // 2
    w_mine = lax.dynamic_index_in_dim(w_chip, z, 0, keepdims=False)
    for k in reversed(range(1, half)):
        block = lax.dynamic_index_in_dim(w_chip, z ^ k, 0, keepdims=False)
        w_mine = w_mine + swap(block.astype(jnp.bfloat16), "ctx", 2 * k).astype(jnp.float32)

    low = w_mine.astype(jnp.bfloat16)
    low, gq = lax.optimization_barrier((low, gq))
    blocks = [low] + [swap(low, "dp", k) for k in range(1, rows)]
    bit = 1
    while bit < rows:
        flip = (row & bit) != 0
        blocks = [jnp.where(flip, blocks[j ^ bit], blocks[j]) for j in range(rows)]
        bit *= 2
    w_out = jnp.concatenate([b.astype(jnp.float32) for b in blocks], axis=0)
    return (
        gq.reshape(1, 1, local, -1),
        gkv.reshape(1, 1, local, 2 * HD),
        w_out,
    )


def solution(mesh):
    spec = P("dp", "ctx", None, None)
    return jax.shard_map(
        on_device,
        mesh=mesh,
        in_specs=(spec, spec, spec, spec, P("dp", None)),
        out_specs=(spec, spec, P("ctx", None)),
        check_vma=False,
    )
```
